256 devices in a mesh: var: 32 (over z, y_lo, core), samp: 8 (over y_hi, x).
Axes of the slice: x: 4, y: 4 (y_hi: 2, y_lo: 2; y = y_hi * 2 + y_lo), z: 8, core: 2. Of those that a mesh axis runs over, the one named last changes fastest.
Arguments:
- dosage: float32 [4096, 8192], P('samp', 'var'), may hold values from 0 to 2, as said below
Outputs:
- ld_stat: float32 [8192, 4096], P('var', 'samp')
The draws below stay inside these ranges and needn't reach their ends.
Inputs may be any that keep to these rules, and one draw needn't show every extreme that they name: `dosage`: dosages of imputed biallelic variants.
All inputs are finite; a program needn't handle non-finite values.
Results may differ from the reference program's by a relative error of at most 0.0003.
Values sent between devices are 32-bit elements; how exact they have to be, the bound alone decides.
A program may use at most 64 MiB of HBM per device.

```python
import jax
import jax.numpy as jnp
from jax import lax

V_DEV = 256
BAND = 4096
VARIANTS = 8192
SAMPLES = 4096


def haplotype_dose(key, founder_allele, frequency, levels, noise_top):
    keys = jax.random.split(key, 9)
    founder_count = founder_allele.shape[0]
    founder = jnp.zeros((SAMPLES, VARIANTS), jnp.int32)
    for level in range(6):
        length = 16 * 2 ** level
        count = (VARIANTS + length - 1) // length
        table = jax.random.randint(keys[level], (SAMPLES, count), 0, founder_count)
        spread = jnp.repeat(table, length, axis=1)[:, :VARIANTS]
        founder = jnp.where(levels[None, :] == level, spread, founder)
    copied = jnp.take_along_axis(founder_allele, founder, axis=0)
    redraw = jax.random.uniform(keys[6], (SAMPLES, VARIANTS), jnp.float32) < 0.3
    fresh = (jax.random.uniform(keys[7], (SAMPLES, VARIANTS), jnp.float32) < frequency).astype(jnp.float32)
    allele = jnp.where(redraw, fresh, copied)
    error = jax.random.uniform(keys[8], (SAMPLES, VARIANTS), jnp.float32, 0.0, noise_top)
    return allele * (1.0 - error) + (1.0 - allele) * error


def draw_dosage(key, part):
    key = jax.random.fold_in(key, 1)
    keys = jax.random.split(key, 5)
    frequency = jax.random.uniform(keys[0], (1, VARIANTS), jnp.float32, 0.05, 0.5)
    noise_top = 0.15
    founder_allele = (jax.random.uniform(keys[1], (8, VARIANTS), jnp.float32) < frequency).astype(jnp.float32)
    levels = jax.random.randint(keys[2], (VARIANTS,), 0, 6)
    first = haplotype_dose(keys[3], founder_allele, frequency, levels, noise_top)
    second = haplotype_dose(keys[4], founder_allele, frequency, levels, noise_top)
    return first + second


def setup_inputs(seed: int = 0) -> dict:
    key_of = jax.random.split(jax.random.key(seed), 2)
    dosage = draw_dosage(jax.random.fold_in(key_of[1], 71), 0)
    return dict(dosage=dosage)


def reference(dosage):
    allele_total = lax.optimization_barrier(jnp.sum(dosage, axis=0))
    allele_square = lax.optimization_barrier(jnp.sum(dosage * dosage, axis=0))
    mean_dose = allele_total / SAMPLES
    inv_scale = lax.rsqrt(allele_square / SAMPLES - mean_dose * mean_dose + 1e-06)
    standard = (dosage - mean_dose) * inv_scale
    padded = jnp.pad(standard, ((0, 0), (0, BAND)))
    span = V_DEV + BAND

    def one_block(index):
        start = (index * V_DEV).astype(jnp.int32)
        zero = jnp.zeros((), jnp.int32)
        rows = lax.dynamic_slice(standard, (zero, start), (SAMPLES, V_DEV))
        extent = lax.dynamic_slice(padded, (zero, start), (SAMPLES, span))
        product = jnp.dot(rows.T, extent, precision=lax.Precision.HIGHEST, preferred_element_type=jnp.float32)
        flattened = jnp.pad(product.reshape(-1), (0, V_DEV))
        return flattened.reshape(V_DEV, span + 1)[:, 1:1 + BAND]
    blocks = lax.map(one_block, jnp.arange(VARIANTS // V_DEV, dtype=jnp.int32))
    scale = 1.0 / jnp.sqrt(jnp.float32(SAMPLES))
    return blocks.reshape(VARIANTS, BAND) * scale
```

```python
import jax
import jax.numpy as jnp
from jax import lax
from jax.experimental import pallas as pl
from jax.experimental.pallas import tpu as pltpu
from jax.sharding import PartitionSpec as P

MESH = pl.DeviceIdType.MESH
SAMPLES = 4096
VARIANTS = 8192
W = 256
K = 512
L = 128
NZ, NX = 8, 4
F32, BF16 = jnp.float32, jnp.bfloat16


def split(a):
    hi = a.astype(BF16)
    return hi, (a - hi.astype(F32)).astype(BF16)


def kernel(
    x_ref, o_ref,
    stat_out, stat_in, cols, rows_in, lhs, gram, part, half_in, full_in, y_in,
    stat_ss, stat_rs, row_ss, row_rs, z_ss, z_rs, sib_ss, sib_rs, x_ss, h_rs, f_rs, y_ss, y_rs,
):
    v, samp = lax.axis_index("var"), lax.axis_index("samp")
    z, yl, c = v // 4, (v // 2) % 2, v % 2
    yh, x = samp // 4, samp % 4

    def device(z=z, yl=yl, c=c, yh=yh, x=x):
        return (z * 4 + yl * 2 + c, yh * 4 + x)

    def remote(src, dst, ss, rs, to):
        return pltpu.make_async_remote_copy(
            src_ref=src, dst_ref=dst, send_sem=ss, recv_sem=rs, device_id=to, device_id_type=MESH
        )

    z_up, z_down = (z + 1) % NZ, (z + NZ - 1) % NZ
    x_right, x_left = (x + 1) % NX, (x + NX - 1) % NX
    sibling = device(c=1 - c)
    peers = [device(yh=(yh + k // 4) % 2, x=(x + k % 4) % NX) for k in range(1, 8)]
    others = [sibling, device(yl=1 - yl), device(yl=1 - yl, yh=1 - yh), device(z=z_up), device(z=z_down)]

    barrier = pltpu.get_barrier_semaphore()
    for to in peers + others:
        pl.semaphore_signal(barrier, inc=1, device_id=to, device_id_type=MESH)

    dose = x_ref[...]
    total = jnp.sum(dose, axis=0, keepdims=True)
    square = jnp.sum(dose * dose, axis=0, keepdims=True)
    line = lax.broadcasted_iota(jnp.int32, (8, W), 0)
    stat_out[...] = jnp.where(line == 0, total, jnp.where(line == 1, square, 0.0))
    pl.semaphore_wait(barrier, len(peers) + len(others))
    stat_copies = [
        remote(stat_out, stat_in.at[k - 1], stat_ss.at[k - 1], stat_rs.at[k - 1], peers[k - 1])
        for k in range(1, 8)
    ]
    for copy in stat_copies:
        copy.start()
    for copy in stat_copies:
        copy.wait_recv()
    sums = stat_out[...]
    for k in range(7):
        sums = sums + stat_in[k]
    mean = sums[0:1] / SAMPLES
    inv = lax.rsqrt(sums[1:2] / SAMPLES - mean * mean + 1e-06)
    standard = (dose - mean) * inv
    for h in range(2):
        cols[0, c, h] = standard[:, h * L : (h + 1) * L]

    def z_copy(dist, h):
        return remote(
            cols.at[dist, c, h], cols.at[dist + 1, c, h], z_ss.at[dist, h], z_rs.at[dist, h], device(z=z_down)
        )

    def sib_copy(dist, h):
        return remote(cols.at[dist, c, h], cols.at[dist, c, h], sib_ss.at[dist, h], sib_rs.at[dist, h], sibling)

    row_copy = remote(cols.at[0, c], rows_in, row_ss, row_rs, device(yl=1 - yl))
    z_copy(0, 0).start()
    row_copy.start()
    z_copy(0, 1).start()
    for h in range(2):
        sib_copy(0, h).start()

    def put_rows(index, first, block):
        hi, lo = split(block)
        spot = (index, pl.ds(first, block.shape[0]))
        lhs[spot + (pl.ds(0, K),)] = hi
        lhs[spot + (pl.ds(K, K),)] = lo
        lhs[spot + (pl.ds(2 * K, K),)] = hi

    put_rows(yl, 0, standard.T)

    def multiply(dist, h):
        right = jnp.concatenate([cols[dist, 0, h], cols[dist, 1, h]], axis=1)
        hi, lo = split(right)
        right = jnp.concatenate([hi, hi, lo], axis=0)
        for r in range(2):
            out = jnp.dot(lhs[r], right, preferred_element_type=F32)
            gram[h, dist, r, 0] = out[:, :L]
            gram[h, dist, r, 1] = out[:, L:]

    row_id = lax.broadcasted_iota(jnp.int32, (W, L), 0)
    lane_id = lax.broadcasted_iota(jnp.int32, (W, L), 1)

    def tile(h, d):
        c2 = (c + d) % 2
        dist = (d - 2 * yl + c + 2) // 4
        r = (yl + 8 * 2 - (d - (c2 - c)) // 2) % 2
        return gram[h, dist, r, c2]

    def build(h, s):
        first = jnp.where(lane_id + h * L > row_id, tile(h, 2 * s), tile(h, 2 * s + 2))
        second = tile(h, 2 * s + 1)
        for p in range(2):
            part[h, s, 0, p] = first[p * L : (p + 1) * L]
            part[h, s, 1, p] = second[p * L : (p + 1) * L]

    def role(s):
        return (s % 4 + NX - x) % NX

    def side(s):
        return (role(s) - 1) // 2

    def far_copy(h, s, p):
        to = device(x=x_right if p == 0 else x_left)
        return remote(part.at[h, s, :, p], half_in.at[h, s], x_ss.at[h, s, p], h_rs.at[h, s], to)

    def near_copy(h, s, p):
        q = side(s)
        to = device(x=(x + 1 + 2 * q) % NX)
        return remote(
            part.at[h, s, :, p], full_in.at[h, s // 4, q, :, p], x_ss.at[h, s, p], f_rs.at[h, s // 4, q, p], to
        )

    def send_first(h, s):
        @pl.when(role(s) == 2)
        def _():
            far_copy(h, s, 0).start()
            far_copy(h, s, 1).start()

        @pl.when(role(s) % 2 == 1)
        def _():
            near_copy(h, s, 1 - side(s)).start()

    def send_second(h, s):
        @pl.when(role(s) % 2 == 1)
        def _():
            p = side(s)
            far_copy(h, s, 0).wait_recv()
            part[h, s, :, p] = part[h, s, :, p] + half_in[h, s]
            near_copy(h, s, p).start()

    def y_copy(h, s, yl2, t):
        me = 2 * yh + yl
        return remote(
            part.at[h, s, t], y_in.at[h, me, t], y_ss.at[h, s // 4, yl2, t], y_rs.at[h, me, t],
            device(yh=s // 4, yl=yl2),
        )

    def to_y(h, s, act):
        for yl2 in range(2):
            away = jnp.logical_or(s // 4 != yh, yl2 != yl)
            wanted = (yl + yl2 + s) % 2 == c

            @pl.when(away)
            def _():
                act(y_copy(h, s, yl2, 0))

            @pl.when(jnp.logical_and(away, wanted))
            def _():
                act(y_copy(h, s, yl2, 1))

    def collect(h, s):
        @pl.when(role(s) == 0)
        def _():
            own = part[h, s]
            for q in range(2):
                for p in range(2):
                    remote(
                        part.at[h, s, :, p], full_in.at[h, s // 4, q, :, p], x_ss.at[h, s, p],
                        f_rs.at[h, s // 4, q, p], device(x=x_right),
                    ).wait_recv()
                own = own + full_in[h, s // 4, q]
            part[h, s] = own
            to_y(h, s, lambda copy: copy.start())

            @pl.when(s // 4 == yh)
            def _():
                y_in[h, 2 * yh + yl] = own

    row_copy.wait_recv()
    for h in range(2):
        put_rows(1 - yl, h * L, rows_in[h].T)
    for h in range(2):
        sib_copy(0, h).wait_recv()
        multiply(0, h)

    steps = [(dist, h) for dist in range(1, 5) for h in range(2)]
    units = [[(h, 2 * dist - 2), (h, 2 * dist - 1)] for dist, h in steps]
    for n, (dist, h) in enumerate(steps):
        z_copy(dist - 1, h).wait_recv()
        if dist < 4:
            z_copy(dist, h).start()
        sib_copy(dist, h).start()
        sib_copy(dist, h).wait_recv()
        multiply(dist, h)
        for unit in units[n]:
            build(*unit)
            send_first(*unit)
        if n >= 1:
            for unit in units[n - 1]:
                send_second(*unit)
        if n >= 2:
            for unit in units[n - 2]:
                collect(*unit)
    for unit in units[-1]:
        send_second(*unit)
    for unit in units[-2] + units[-1]:
        collect(*unit)

    me = 2 * yh + yl
    first_yl = (yl + x) % 2
    mid_yl = (yl + x + c) % 2
    pieces = [[None, None], [None, None]]
    for h in range(2):
        for src in range(4):
            @pl.when(me != src)
            def _():
                remote(part.at[h, 0, 0], y_in.at[h, src, 0], y_ss.at[h, 0, 0, 0], y_rs.at[h, src, 0], sibling).wait_recv()

                @pl.when((src % 2 + yl + x) % 2 == c)
                def _():
                    remote(
                        part.at[h, 0, 1], y_in.at[h, src, 1], y_ss.at[h, 0, 0, 1], y_rs.at[h, src, 1], sibling
                    ).wait_recv()

        upper = (y_in[h, first_yl, 0] + y_in[h, 2 + first_yl, 0]).reshape(W, L)
        lower = (y_in[h, 1 - first_yl, 0] + y_in[h, 3 - first_yl, 0]).reshape(W, L)
        pieces[0][h] = jnp.where(lane_id + h * L > row_id, upper, lower)
        pieces[1][h] = (y_in[h, mid_yl, 1] + y_in[h, 2 + mid_yl, 1]).reshape(W, L)
    band = jnp.concatenate(pieces[0] + pieces[1], axis=1) * (1.0 / 64.0)
    row = lax.broadcasted_iota(jnp.int32, (W, 2 * W), 0)
    shift = row + 1
    for bit in range(9):
        moved = pltpu.roll(band, 2 * W - 2**bit, 1)
        band = jnp.where((shift // 2**bit) % 2 == 1, moved, band)
    reach = v * W + row + 1 + samp * 2 * W + lax.broadcasted_iota(jnp.int32, (W, 2 * W), 1)
    o_ref[...] = jnp.where(reach < VARIANTS, band, 0.0)

    for copy in stat_copies:
        copy.wait_send()
    row_copy.wait_send()
    for h in range(2):
        for dist in range(5):
            if dist < 4:
                z_copy(dist, h).wait_send()
            sib_copy(dist, h).wait_send()
        for s in range(8):
            @pl.when(role(s) != 0)
            def _():
                for p in range(2):
                    far_copy(h, s, p).wait_send()

            @pl.when(role(s) == 0)
            def _():
                to_y(h, s, lambda copy: copy.wait_send())


def body(dosage):
    dma = pltpu.SemaphoreType.DMA
    return pl.pallas_call(
        kernel,
        out_shape=jax.ShapeDtypeStruct((W, 2 * W), F32),
        in_specs=[pl.BlockSpec(memory_space=pltpu.VMEM)],
        out_specs=pl.BlockSpec(memory_space=pltpu.VMEM),
        scratch_shapes=[
            pltpu.VMEM((8, W), F32),
            pltpu.VMEM((7, 8, W), F32),
            pltpu.VMEM((5, 2, 2, K, L), F32),
            pltpu.VMEM((2, K, L), F32),
            pltpu.VMEM((2, W, 3 * K), BF16),
            pltpu.VMEM((2, 5, 2, 2, W, L), F32),
            pltpu.VMEM((2, 8, 2, 2, L, L), F32),
            pltpu.VMEM((2, 8, 2, L, L), F32),
            pltpu.VMEM((2, 2, 2, 2, 2, L, L), F32),
            pltpu.VMEM((2, 4, 2, 2, L, L), F32),
            dma((7,)), dma((7,)),
            dma, dma,
            dma((4, 2)), dma((4, 2)),
            dma((5, 2)), dma((5, 2)),
            dma((2, 8, 2)), dma((2, 8)), dma((2, 2, 2, 2)),
            dma((2, 2, 2, 2)), dma((2, 4, 2)),
        ],
        compiler_params=pltpu.CompilerParams(
            collective_id=0, has_side_effects=True, vmem_limit_bytes=48 * 2**20
        ),
        cost_estimate=pl.CostEstimate(flops=2 * 17 * W * W * K * 3, bytes_accessed=2**20, transcendentals=W),
    )(dosage)


def solution(mesh):
    return jax.shard_map(
        body, mesh=mesh, in_specs=(P("samp", "var"),), out_specs=P("var", "samp"), check_vma=False
    )
```

```python
import jax
import jax.numpy as jnp
from jax import lax
from jax.experimental import pallas as pl
from jax.experimental.pallas import tpu as pltpu
from jax.sharding import PartitionSpec as P

MESH = pl.DeviceIdType.MESH
SAMPLES = 4096
VARIANTS = 8192
W = 256
K = 512
L = 128
NZ, NX = 8, 4
NP = 2
KP = K // NP
F32, BF16 = jnp.float32, jnp.bfloat16


def split(a):
    hi = a.astype(BF16)
    return hi, (a - hi.astype(F32)).astype(BF16)


def kernel(
    x_ref, o_ref,
    stat_out, stat_in, stat, row_stat, cols, rows_in, relay, lhs, gram, part, half_in, full_in, y_in,
    stat_ss, stat_rs, zt_ss, zt_rs, st_ss, st_rs, rt_ss, rt_rs,
    row_ss, row_rs, z_ss, z_rs, far_ss, far_rs, sib_ss, sib_rs, x_ss, h_rs, f_rs, y_ss, y_rs,
):
    v, samp = lax.axis_index("var"), lax.axis_index("samp")
    z, yl, c = v // 4, (v // 2) % 2, v % 2
    yh, x = samp // 4, samp % 4

    def device(z=z, yl=yl, c=c, yh=yh, x=x):
        return (z * 4 + yl * 2 + c, yh * 4 + x)

    def remote(src, dst, ss, rs, to):
        return pltpu.make_async_remote_copy(
            src_ref=src, dst_ref=dst, send_sem=ss, recv_sem=rs, device_id=to, device_id_type=MESH
        )

    z_up, z_down = (z + 1) % NZ, (z + NZ - 1) % NZ
    x_right, x_left = (x + 1) % NX, (x + NX - 1) % NX
    sibling = device(c=1 - c)
    peers = [device(yh=(yh + k // 4) % 2, x=(x + k % 4) % NX) for k in range(1, 8)]
    others = [sibling, device(yl=1 - yl), device(yl=1 - yl, yh=1 - yh), device(z=z_up), device(z=z_down)]
    others += [device(z=(z + 2) % NZ), device(z=(z + 6) % NZ)]

    barrier = pltpu.get_barrier_semaphore()
    for to in peers + others:
        pl.semaphore_signal(barrier, inc=1, device_id=to, device_id_type=MESH)

    def raw(h, first=0, count=K):
        return x_ref.at[pl.ds(first, count), pl.ds(h * L, L)]

    def z_copy(dist, h, p):
        here = pl.ds(p * KP, KP)
        src = cols.at[dist, c, h, here] if dist else raw(h, p * KP, KP)
        return remote(
            src, cols.at[dist + 1, c, h, here], z_ss.at[dist, h, p], z_rs.at[dist, h, p], device(z=z_down)
        )

    def far_copy(hop, h, p):
        here = pl.ds(p * KP, KP)
        src = relay.at[h, here] if hop else raw(h, p * KP, KP)
        dst = cols.at[4, c, h, here] if hop else relay.at[h, here]
        return remote(src, dst, far_ss.at[hop, h, p], far_rs.at[hop, h, p], device(z=(z + 2) % NZ))

    def sib_copy(dist, h):
        there = cols.at[dist, c, h]
        return remote(there if dist else raw(h), there, sib_ss.at[dist, h], sib_rs.at[dist, h], sibling)

    def row_copy(h):
        return remote(raw(h), rows_in.at[h], row_ss.at[h], row_rs.at[h], device(yl=1 - yl))

    def z_stat(dist):
        return remote(
            stat.at[dist, c], stat.at[dist + 1, c], zt_ss.at[dist], zt_rs.at[dist], device(z=z_down)
        )

    def sib_stat(dist):
        return remote(stat.at[dist, c], stat.at[dist, c], st_ss.at[dist], st_rs.at[dist], sibling)

    row_stat_copy = remote(stat.at[0, c], row_stat, rt_ss, rt_rs, device(yl=1 - yl))

    def by_far(h, p):
        return h == 0 or p == 0

    dose = x_ref[...]
    total = jnp.sum(dose, axis=0, keepdims=True)
    square = jnp.sum(dose * dose, axis=0, keepdims=True)
    line = lax.broadcasted_iota(jnp.int32, (8, W), 0)
    stat_out[...] = jnp.where(line == 0, total, jnp.where(line == 1, square, 0.0))
    stat_copies = [
        remote(stat_out, stat_in.at[k - 1], stat_ss.at[k - 1], stat_rs.at[k - 1], peers[k - 1])
        for k in range(1, 8)
    ]
    pl.semaphore_wait(barrier, len(peers) + len(others))
    for copy in stat_copies:
        copy.start()
    row_copy(0).start()
    for p in range(NP):
        z_copy(0, 0, p).start()
    for p in range(NP):
        far_copy(0, 0, p).start()
    for h in range(2):
        sib_copy(0, h).start()
        cols[0, c, h] = dose[:, h * L : (h + 1) * L]
    for copy in stat_copies:
        copy.wait_recv()
    sums = stat_out[...]
    for k in range(7):
        sums = sums + stat_in[k]
    mean = sums[0:1] / SAMPLES
    inv = lax.rsqrt(sums[1:2] / SAMPLES - mean * mean + 1e-06)
    stat[0, c] = jnp.where(line == 0, mean, inv)
    z_stat(0).start()
    row_stat_copy.start()
    sib_stat(0).start()
    row_copy(1).start()
    for p in range(NP):
        z_copy(0, 1, p).start()
        if by_far(1, p):
            far_copy(0, 1, p).start()

    def put_rows(index, first, block):
        hi, lo = split(block)
        spot = (index, pl.ds(first, block.shape[0]))
        lhs[spot + (pl.ds(0, K),)] = hi
        lhs[spot + (pl.ds(K, K),)] = lo
        lhs[spot + (pl.ds(2 * K, K),)] = hi

    put_rows(yl, 0, ((dose - mean) * inv).T)

    def multiply(dist, h):
        right = []
        for c2 in range(2):
            of = stat[dist, c2, :, h * L : (h + 1) * L]
            right.append((cols[dist, c2, h] - of[0:1]) * of[1:2])
        right = jnp.concatenate(right, axis=1)
        hi, lo = split(right)
        right = jnp.concatenate([hi, hi, lo], axis=0)
        for r in range(2):
            out = jnp.dot(lhs[r], right, preferred_element_type=F32)
            gram[h, dist, r, 0] = out[:, :L]
            gram[h, dist, r, 1] = out[:, L:]

    row_id = lax.broadcasted_iota(jnp.int32, (W, L), 0)
    lane_id = lax.broadcasted_iota(jnp.int32, (W, L), 1)

    def tile(h, d):
        c2 = (c + d) % 2
        dist = (d - 2 * yl + c + 2) // 4
        r = (yl + 8 * 2 - (d - (c2 - c)) // 2) % 2
        return gram[h, dist, r, c2]

    def build(h, s):
        first = jnp.where(lane_id + h * L > row_id, tile(h, 2 * s), tile(h, 2 * s + 2))
        second = tile(h, 2 * s + 1)
        for p in range(2):
            part[h, s, 0, p] = first[p * L : (p + 1) * L]
            part[h, s, 1, p] = second[p * L : (p + 1) * L]

    def role(s):
        return (s % 4 + NX - x) % NX

    def side(s):
        return (role(s) - 1) // 2

    def far_half(h, s, p):
        to = device(x=x_right if p == 0 else x_left)
        return remote(part.at[h, s, :, p], half_in.at[h, s], x_ss.at[h, s, p], h_rs.at[h, s], to)

    def near_copy(h, s, p):
        q = side(s)
        to = device(x=(x + 1 + 2 * q) % NX)
        return remote(
            part.at[h, s, :, p], full_in.at[h, s // 4, q, :, p], x_ss.at[h, s, p], f_rs.at[h, s // 4, q, p], to
        )

    def send_first(group):
        for h, s in group:
            @pl.when(role(s) == 2)
            def _():
                build(h, s)
                far_half(h, s, 0).start()
                far_half(h, s, 1).start()

        for h, s in group:
            @pl.when(role(s) % 2 == 1)
            def _():
                build(h, s)
                near_copy(h, s, 1 - side(s)).start()

        for h, s in group:
            @pl.when(role(s) == 0)
            def _():
                build(h, s)

    def send_second(h, s):
        @pl.when(role(s) % 2 == 1)
        def _():
            p = side(s)
            far_half(h, s, 0).wait_recv()
            part[h, s, :, p] = part[h, s, :, p] + half_in[h, s]
            near_copy(h, s, p).start()

    def y_copy(h, s, yl2, t):
        me = 2 * yh + yl
        return remote(
            part.at[h, s, t], y_in.at[h, me, t], y_ss.at[h, s // 4, yl2, t], y_rs.at[h, me, t],
            device(yh=s // 4, yl=yl2),
        )

    def to_y(h, s, act):
        for yl2 in range(2):
            away = jnp.logical_or(s // 4 != yh, yl2 != yl)
            wanted = (yl + yl2 + s) % 2 == c

            @pl.when(away)
            def _():
                act(y_copy(h, s, yl2, 0))

            @pl.when(jnp.logical_and(away, wanted))
            def _():
                act(y_copy(h, s, yl2, 1))

    def collect(h, s):
        @pl.when(role(s) == 0)
        def _():
            own = part[h, s]
            for q in range(2):
                for p in range(2):
                    remote(
                        part.at[h, s, :, p], full_in.at[h, s // 4, q, :, p], x_ss.at[h, s, p],
                        f_rs.at[h, s // 4, q, p], device(x=x_right),
                    ).wait_recv()
                own = own + full_in[h, s // 4, q]
            part[h, s] = own
            to_y(h, s, lambda copy: copy.start())

            @pl.when(s // 4 == yh)
            def _():
                y_in[h, 2 * yh + yl] = own

    steps = [(1, 0), (1, 1), (2, 0), (2, 1), (3, 0), (4, 0), (3, 1), (4, 1)]
    units = [[(h, 2 * dist - 2), (h, 2 * dist - 1)] for dist, h in steps]

    def receive(n):
        dist, h = steps[n]
        if h == 0:
            z_stat(dist - 1).wait_recv()
            if dist < 4:
                z_stat(dist).start()
            sib_stat(dist).start()
        for p in range(NP):
            if dist == 4 and by_far(h, p):
                far_copy(1, h, p).wait_recv()
            else:
                z_copy(dist - 1, h, p).wait_recv()
            if dist < 3 or (dist == 3 and not by_far(h, p)):
                z_copy(dist, h, p).start()
        sib_copy(dist, h).start()

    def pass_on(h):
        for p in range(NP):
            if by_far(h, p):
                far_copy(0, h, p).wait_recv()
                far_copy(1, h, p).start()

    def work(n):
        dist, h = steps[n]
        if dist == 1:
            if h == 0:
                sib_stat(0).wait_recv()
            sib_copy(0, h).wait_recv()
            multiply(0, h)
        if h == 0:
            sib_stat(dist).wait_recv()
        sib_copy(dist, h).wait_recv()
        multiply(dist, h)
        send_first(units[n])

    def second(n):
        for unit in units[n]:
            send_second(*unit)

    def gather(n):
        for unit in units[n]:
            collect(*unit)

    receive(0)
    row_stat_copy.wait_recv()
    for h in range(2):
        row_copy(h).wait_recv()
        of = row_stat[:, h * L : (h + 1) * L]
        put_rows(1 - yl, h * L, ((rows_in[h] - of[0:1]) * of[1:2]).T)
    receive(1)
    work(0)
    pass_on(0)
    work(1)
    receive(2)
    second(0)
    second(1)
    work(2)
    receive(3)
    second(2)
    work(3)
    pass_on(1)
    gather(0)
    gather(1)
    receive(4)
    second(3)
    work(4)
    receive(5)
    work(5)
    gather(2)
    receive(6)
    second(4)
    second(5)
    work(6)
    gather(3)
    receive(7)
    second(6)
    work(7)
    gather(4)
    gather(5)
    second(7)
    gather(6)
    gather(7)

    me = 2 * yh + yl
    first_yl = (yl + x) % 2
    mid_yl = (yl + x + c) % 2
    pieces = [[None, None], [None, None]]
    for h in range(2):
        for src in range(4):
            @pl.when(me != src)
            def _():
                remote(part.at[h, 0, 0], y_in.at[h, src, 0], y_ss.at[h, 0, 0, 0], y_rs.at[h, src, 0], sibling).wait_recv()

                @pl.when((src % 2 + yl + x) % 2 == c)
                def _():
                    remote(
                        part.at[h, 0, 1], y_in.at[h, src, 1], y_ss.at[h, 0, 0, 1], y_rs.at[h, src, 1], sibling
                    ).wait_recv()

        upper = (y_in[h, first_yl, 0] + y_in[h, 2 + first_yl, 0]).reshape(W, L)
        lower = (y_in[h, 1 - first_yl, 0] + y_in[h, 3 - first_yl, 0]).reshape(W, L)
        pieces[0][h] = jnp.where(lane_id + h * L > row_id, upper, lower)
        pieces[1][h] = (y_in[h, mid_yl, 1] + y_in[h, 2 + mid_yl, 1]).reshape(W, L)
    band = jnp.concatenate(pieces[0] + pieces[1], axis=1) * (1.0 / 64.0)
    row = lax.broadcasted_iota(jnp.int32, (W, 2 * W), 0)
    shift = row + 1
    for bit in range(9):
        moved = pltpu.roll(band, 2 * W - 2**bit, 1)
        band = jnp.where((shift // 2**bit) % 2 == 1, moved, band)
    reach = v * W + row + 1 + samp * 2 * W + lax.broadcasted_iota(jnp.int32, (W, 2 * W), 1)
    o_ref[...] = jnp.where(reach < VARIANTS, band, 0.0)

    for copy in stat_copies:
        copy.wait_send()
    row_stat_copy.wait_send()
    for dist in range(5):
        if dist < 4:
            z_stat(dist).wait_send()
        sib_stat(dist).wait_send()
    for h in range(2):
        row_copy(h).wait_send()
        for p in range(NP):
            for dist in range(3):
                z_copy(dist, h, p).wait_send()
            if by_far(h, p):
                far_copy(0, h, p).wait_send()
                far_copy(1, h, p).wait_send()
            else:
                z_copy(3, h, p).wait_send()
        for dist in range(5):
            sib_copy(dist, h).wait_send()
        for s in range(8):
            @pl.when(role(s) != 0)
            def _():
                for p in range(2):
                    far_half(h, s, p).wait_send()

            @pl.when(role(s) == 0)
            def _():
                to_y(h, s, lambda copy: copy.wait_send())


def body(dosage):
    dma = pltpu.SemaphoreType.DMA
    return pl.pallas_call(
        kernel,
        out_shape=jax.ShapeDtypeStruct((W, 2 * W), F32),
        in_specs=[pl.BlockSpec(memory_space=pltpu.VMEM)],
        out_specs=pl.BlockSpec(memory_space=pltpu.VMEM),
        scratch_shapes=[
            pltpu.VMEM((8, W), F32),
            pltpu.VMEM((7, 8, W), F32),
            pltpu.VMEM((5, 2, 8, W), F32),
            pltpu.VMEM((8, W), F32),
            pltpu.VMEM((5, 2, 2, K, L), F32),
            pltpu.VMEM((2, K, L), F32),
            pltpu.VMEM((2, K, L), F32),
            pltpu.VMEM((2, W, 3 * K), BF16),
            pltpu.VMEM((2, 5, 2, 2, W, L), F32),
            pltpu.VMEM((2, 8, 2, 2, L, L), F32),
            pltpu.VMEM((2, 8, 2, L, L), F32),
            pltpu.VMEM((2, 2, 2, 2, 2, L, L), F32),
            pltpu.VMEM((2, 4, 2, 2, L, L), F32),
            dma((7,)), dma((7,)),
            dma((4,)), dma((4,)), dma((5,)), dma((5,)), dma, dma,
            dma((2,)), dma((2,)), dma((4, 2, NP)), dma((4, 2, NP)), dma((2, 2, NP)), dma((2, 2, NP)),
            dma((5, 2)), dma((5, 2)),
            dma((2, 8, 2)), dma((2, 8)), dma((2, 2, 2, 2)),
            dma((2, 2, 2, 2)), dma((2, 4, 2)),
        ],
        compiler_params=pltpu.CompilerParams(
            collective_id=0, has_side_effects=True, vmem_limit_bytes=48 * 2**20
        ),
        cost_estimate=pl.CostEstimate(flops=2 * 17 * W * W * K * 3, bytes_accessed=2**20, transcendentals=W),
    )(dosage)


def solution(mesh):
    return jax.shard_map(
        body, mesh=mesh, in_specs=(P("samp", "var"),), out_specs=P("var", "samp"), check_vma=False
    )
```

```python
import jax
import jax.numpy as jnp
from jax import lax
from jax.experimental import pallas as pl
from jax.experimental.pallas import tpu as pltpu
from jax.sharding import PartitionSpec as P

MESH = pl.DeviceIdType.MESH
SAMPLES = 4096
VARIANTS = 8192
W = 256
K = 512
L = 128
NZ, NX = 8, 4
NP = 2
KP = K // NP
F32, BF16 = jnp.float32, jnp.bfloat16
STEPS = ((1, 0), (2, 0), (3, 0), (1, 1), (4, 0), (2, 1), (3, 1), (4, 1))
ORDER = (
    "H", "Y0", "R0", "Y1", "M00", "M01", "R3", "M30", "P0", "F01", "R1", "M10", "O10", "O00", "F30", "F00",
    "F10", "M11", "S10", "P1", "O30", "M31", "O11", "O01", "O31", "R5", "S00", "M50", "F50", "O50", "F11",
    "M51", "S01", "O51", "R2", "R4", "M20", "F51", "S30", "M21", "O20", "G10", "M40", "G00", "S51", "F21",
    "O21", "F31", "M41", "O40", "F40", "R6", "O41", "M60", "S21", "F41", "R7", "F20", "G51", "S40", "M61",
    "M70", "O70", "O60", "S41", "G21", "S20", "F70", "F60", "S50", "G40", "S60", "M71", "G30", "F61", "O61",
    "O71", "G01", "G20", "S31", "G41", "S70", "G60", "S11", "G50", "F71", "S71", "S61", "G70", "G11", "G61",
    "G31", "G71",
)


def split(a):
    hi = a.astype(BF16)
    return hi, (a - hi.astype(F32)).astype(BF16)


def kernel(
    x_ref, o_ref,
    stat_out, stat_in, stat, row_stat, cols, rows_in, relay, lhs, gram, part, half_in, full_in, y_in,
    stat_ss, stat_rs, zt_ss, zt_rs, st_ss, st_rs, rt_ss, rt_rs,
    row_ss, row_rs, z_ss, z_rs, far_ss, far_rs, sib_ss, sib_rs, x_ss, h_rs, f_rs, y_ss, y_rs,
):
    v, samp = lax.axis_index("var"), lax.axis_index("samp")
    z, yl, c = v // 4, (v // 2) % 2, v % 2
    yh, x = samp // 4, samp % 4

    def device(z=z, yl=yl, c=c, yh=yh, x=x):
        return (z * 4 + yl * 2 + c, yh * 4 + x)

    def remote(src, dst, ss, rs, to):
        return pltpu.make_async_remote_copy(
            src_ref=src, dst_ref=dst, send_sem=ss, recv_sem=rs, device_id=to, device_id_type=MESH
        )

    z_up, z_down = (z + 1) % NZ, (z + NZ - 1) % NZ
    x_right, x_left = (x + 1) % NX, (x + NX - 1) % NX
    sibling = device(c=1 - c)
    peers = [device(yh=(yh + k // 4) % 2, x=(x + k % 4) % NX) for k in range(1, 8)]
    others = [sibling, device(yl=1 - yl), device(yl=1 - yl, yh=1 - yh), device(z=z_up), device(z=z_down)]
    others += [device(z=(z + 2) % NZ), device(z=(z + 6) % NZ)]

    barrier = pltpu.get_barrier_semaphore()
    for to in peers + others:
        pl.semaphore_signal(barrier, inc=1, device_id=to, device_id_type=MESH)

    def raw(h, first=0, count=K):
        return cols.at[0, c, h, pl.ds(first, count)]

    def z_copy(dist, h, p):
        here = pl.ds(p * KP, KP)
        src = cols.at[dist, c, h, here] if dist else raw(h, p * KP, KP)
        return remote(
            src, cols.at[dist + 1, c, h, here], z_ss.at[dist, h, p], z_rs.at[dist, h, p], device(z=z_down)
        )

    def far_copy(hop, h, p):
        here = pl.ds(p * KP, KP)
        src = relay.at[h, here] if hop else raw(h, p * KP, KP)
        dst = cols.at[4, c, h, here] if hop else relay.at[h, here]
        return remote(src, dst, far_ss.at[hop, h, p], far_rs.at[hop, h, p], device(z=(z + 2) % NZ))

    def sib_copy(dist, h):
        there = cols.at[dist, c, h]
        return remote(there if dist else raw(h), there, sib_ss.at[dist, h], sib_rs.at[dist, h], sibling)

    def row_copy(h):
        return remote(raw(h), rows_in.at[h], row_ss.at[h], row_rs.at[h], device(yl=1 - yl))

    def z_stat(dist):
        return remote(
            stat.at[dist, c], stat.at[dist + 1, c], zt_ss.at[dist], zt_rs.at[dist], device(z=z_down)
        )

    def sib_stat(dist):
        return remote(stat.at[dist, c], stat.at[dist, c], st_ss.at[dist], st_rs.at[dist], sibling)

    row_stat_copy = remote(stat.at[0, c], row_stat, rt_ss, rt_rs, device(yl=1 - yl))

    def by_far(h, p):
        return h == 0 or p == 0

    dose = x_ref[...]
    for h in range(2):
        cols[0, c, h] = dose[:, h * L : (h + 1) * L]
    total = jnp.sum(dose, axis=0, keepdims=True)
    square = jnp.sum(dose * dose, axis=0, keepdims=True)
    line = lax.broadcasted_iota(jnp.int32, (8, W), 0)
    stat_out[...] = jnp.where(line == 0, total, jnp.where(line == 1, square, 0.0))
    stat_copies = [
        remote(stat_out, stat_in.at[k - 1], stat_ss.at[k - 1], stat_rs.at[k - 1], peers[k - 1])
        for k in range(1, 8)
    ]
    pl.semaphore_wait(barrier, len(peers) + len(others))
    for copy in stat_copies:
        copy.start()
    row_copy(0).start()
    for p in range(NP):
        z_copy(0, 0, p).start()
    for p in range(NP):
        far_copy(0, 0, p).start()
    for h in range(2):
        sib_copy(0, h).start()
    for copy in stat_copies:
        copy.wait_recv()
    sums = stat_out[...]
    for k in range(7):
        sums = sums + stat_in[k]
    mean = sums[0:1] / SAMPLES
    inv = lax.rsqrt(sums[1:2] / SAMPLES - mean * mean + 1e-06)
    stat[0, c] = jnp.where(line == 0, mean, inv)
    z_stat(0).start()
    row_stat_copy.start()
    sib_stat(0).start()
    row_copy(1).start()

    def put_rows(index, first, block):
        hi, lo = split(block)
        spot = (index, pl.ds(first, block.shape[0]))
        lhs[spot + (pl.ds(0, K),)] = hi
        lhs[spot + (pl.ds(K, K),)] = lo
        lhs[spot + (pl.ds(2 * K, K),)] = hi

    put_rows(yl, 0, ((dose - mean) * inv).T)

    def multiply(dist, h, p):
        right = []
        for c2 in range(2):
            of = stat[dist, c2, :, h * L : (h + 1) * L]
            right.append((cols[dist, c2, h] - of[0:1]) * of[1:2])
        hi, lo = split(jnp.concatenate(right, axis=1))
        right = jnp.concatenate([hi, hi, lo], axis=0)
        rows = pl.ds(p * L, L)
        for r in range(2):
            out = jnp.dot(lhs[r, rows], right, preferred_element_type=F32)
            gram[h, dist, r, 0, rows] = out[:, :L]
            gram[h, dist, r, 1, rows] = out[:, L:]

    row_id = lax.broadcasted_iota(jnp.int32, (L, L), 0)
    lane_id = lax.broadcasted_iota(jnp.int32, (L, L), 1)

    def tile(h, d, p):
        c2 = (c + d) % 2
        dist = (d - 2 * yl + c + 2) // 4
        r = (yl + 8 * 2 - (d - (c2 - c)) // 2) % 2
        return gram[h, dist, r, c2, pl.ds(p * L, L)]

    def build(h, s, p):
        above = lane_id + h * L > row_id + p * L
        part[h, s, p, 0] = jnp.where(above, tile(h, 2 * s, p), tile(h, 2 * s + 2, p))
        part[h, s, p, 1] = tile(h, 2 * s + 1, p)

    def role(s):
        return (s % 4 + NX - x) % NX

    def side(s):
        return (role(s) - 1) // 2

    def far_half(h, s, p, t):
        to = device(x=x_right if t == 0 else x_left)
        return remote(part.at[h, s, p, t], half_in.at[h, s, p], x_ss.at[h, s, p, t], h_rs.at[h, s, p], to)

    def near_copy(h, s, p, t):
        q = side(s)
        to = device(x=(x + 1 + 2 * q) % NX)
        return remote(
            part.at[h, s, p, t], full_in.at[h, s // 4, q, p, t], x_ss.at[h, s, p, t], f_rs.at[h, s // 4, q, p, t], to
        )

    def send_opposite(h, s, p):
        @pl.when(role(s) == 2)
        def _():
            build(h, s, p)
            far_half(h, s, p, 0).start()
            far_half(h, s, p, 1).start()

    def send_free(h, s, p):
        @pl.when(role(s) % 2 == 1)
        def _():
            build(h, s, p)
            near_copy(h, s, p, 1 - side(s)).start()

    def send_second(h, s, p):
        @pl.when(role(s) % 2 == 1)
        def _():
            t = side(s)
            far_half(h, s, p, 0).wait_recv()
            part[h, s, p, t] = part[h, s, p, t] + half_in[h, s, p]
            near_copy(h, s, p, t).start()

    def y_copy(h, s, yl2, p, t):
        me = 2 * yh + yl
        return remote(
            part.at[h, s, p, t], y_in.at[h, me, p, t], y_ss.at[h, s // 4, yl2, p, t], y_rs.at[h, me, p, t],
            device(yh=s // 4, yl=yl2),
        )

    def to_y(h, s, p, act):
        for yl2 in range(2):
            away = jnp.logical_or(s // 4 != yh, yl2 != yl)
            wanted = (yl + yl2 + s) % 2 == c

            @pl.when(away)
            def _():
                act(y_copy(h, s, yl2, p, 0))

            @pl.when(jnp.logical_and(away, wanted))
            def _():
                act(y_copy(h, s, yl2, p, 1))

    def collect(h, s, p):
        @pl.when(role(s) == 0)
        def _():
            build(h, s, p)
            for t in range(2):
                for q in range(2):
                    remote(
                        part.at[h, s, p, t], full_in.at[h, s // 4, q, p, t], x_ss.at[h, s, p, t],
                        f_rs.at[h, s // 4, q, p, t], device(x=x_right),
                    ).wait_recv()
                part[h, s, p, t] = part[h, s, p, t] + full_in[h, s // 4, 0, p, t] + full_in[h, s // 4, 1, p, t]
            to_y(h, s, p, lambda copy: copy.start())

            @pl.when(s // 4 == yh)
            def _():
                y_in[h, 2 * yh + yl, p] = part[h, s, p]

    def start_half():
        for p in range(NP):
            z_copy(0, 1, p).start()
            if by_far(1, p):
                far_copy(0, 1, p).start()

    def other_rows(p):
        if p == 0:
            row_stat_copy.wait_recv()
        row_copy(p).wait_recv()
        of = row_stat[:, p * L : (p + 1) * L]
        put_rows(1 - yl, p * L, ((rows_in[p] - of[0:1]) * of[1:2]).T)

    def receive(n):
        dist, h = STEPS[n]
        if h == 0:
            z_stat(dist - 1).wait_recv()
            if dist < 4:
                z_stat(dist).start()
            sib_stat(dist).start()
        for p in range(NP):
            if dist == 4 and by_far(h, p):
                far_copy(1, h, p).wait_recv()
            else:
                z_copy(dist - 1, h, p).wait_recv()
            if dist < 3 or (dist == 3 and not by_far(h, p)):
                z_copy(dist, h, p).start()
        sib_copy(dist, h).start()

    def pass_on(h):
        for p in range(NP):
            if by_far(h, p):
                far_copy(0, h, p).wait_recv()
                far_copy(1, h, p).start()

    def work(n, p):
        dist, h = STEPS[n]
        if p == 0:
            if dist == 1:
                if h == 0:
                    sib_stat(0).wait_recv()
                sib_copy(0, h).wait_recv()
            if h == 0:
                sib_stat(dist).wait_recv()
            sib_copy(dist, h).wait_recv()
        if dist == 1:
            multiply(0, h, p)
        multiply(dist, h, p)

    parts = dict(H=start_half, R=receive, P=pass_on, Y=other_rows, M=work)
    each = dict(O=send_opposite, F=send_free, S=send_second, G=collect)
    for event in ORDER:
        kind, digits = event[0], [int(digit) for digit in event[1:]]
        if kind in parts:
            parts[kind](*digits)
        else:
            dist, h = STEPS[digits[0]]
            for unit in (2 * dist - 2, 2 * dist - 1):
                each[kind](h, unit, digits[1])

    me = 2 * yh + yl
    first_yl = (yl + x) % 2
    mid_yl = (yl + x + c) % 2

    def landed(h, src, p, t):
        return remote(
            part.at[h, 0, p, t], y_in.at[h, src, p, t], y_ss.at[h, 0, 0, p, t], y_rs.at[h, src, p, t], sibling
        )

    row = lax.broadcasted_iota(jnp.int32, (L, 2 * W), 0)
    lane = lax.broadcasted_iota(jnp.int32, (L, 2 * W), 1)
    for p in range(2):
        pieces = [[None, None], [None, None]]
        for h in range(2):
            for src in range(4):
                @pl.when(me != src)
                def _():
                    landed(h, src, p, 0).wait_recv()

                    @pl.when((src % 2 + yl + x) % 2 == c)
                    def _():
                        landed(h, src, p, 1).wait_recv()

            upper = y_in[h, first_yl, p, 0] + y_in[h, 2 + first_yl, p, 0]
            lower = y_in[h, 1 - first_yl, p, 0] + y_in[h, 3 - first_yl, p, 0]
            pieces[0][h] = jnp.where(lane_id + h * L > row_id + p * L, upper, lower)
            pieces[1][h] = y_in[h, mid_yl, p, 1] + y_in[h, 2 + mid_yl, p, 1]
        band = jnp.concatenate(pieces[0] + pieces[1], axis=1) * (1.0 / 64.0)
        shift = row + (p * L + 1)
        for bit in range(9):
            moved = pltpu.roll(band, 2 * W - 2**bit, 1)
            band = jnp.where((shift & 2**bit) != 0, moved, band)
        reach = v * W + shift + samp * 2 * W + lane
        o_ref[p * L : (p + 1) * L] = jnp.where(reach < VARIANTS, band, 0.0)

    for copy in stat_copies:
        copy.wait_send()
    row_stat_copy.wait_send()
    for dist in range(5):
        if dist < 4:
            z_stat(dist).wait_send()
        sib_stat(dist).wait_send()
    for h in range(2):
        row_copy(h).wait_send()
        for p in range(NP):
            for dist in range(3):
                z_copy(dist, h, p).wait_send()
            if by_far(h, p):
                far_copy(0, h, p).wait_send()
                far_copy(1, h, p).wait_send()
            else:
                z_copy(3, h, p).wait_send()
        for dist in range(5):
            sib_copy(dist, h).wait_send()
        for s in range(8):
            @pl.when(role(s) != 0)
            def _():
                for p in range(2):
                    for t in range(2):
                        far_half(h, s, p, t).wait_send()

            @pl.when(role(s) == 0)
            def _():
                for p in range(2):
                    to_y(h, s, p, lambda copy: copy.wait_send())


def body(dosage):
    dma = pltpu.SemaphoreType.DMA
    return pl.pallas_call(
        kernel,
        out_shape=jax.ShapeDtypeStruct((W, 2 * W), F32),
        in_specs=[pl.BlockSpec(memory_space=pltpu.VMEM)],
        out_specs=pl.BlockSpec(memory_space=pltpu.VMEM),
        scratch_shapes=[
            pltpu.VMEM((8, W), F32),
            pltpu.VMEM((7, 8, W), F32),
            pltpu.VMEM((5, 2, 8, W), F32),
            pltpu.VMEM((8, W), F32),
            pltpu.VMEM((5, 2, 2, K, L), F32),
            pltpu.VMEM((2, K, L), F32),
            pltpu.VMEM((2, K, L), F32),
            pltpu.VMEM((2, W, 3 * K), BF16),
            pltpu.VMEM((2, 5, 2, 2, W, L), F32),
            pltpu.VMEM((2, 8, 2, 2, L, L), F32),
            pltpu.VMEM((2, 8, 2, L, L), F32),
            pltpu.VMEM((2, 2, 2, 2, 2, L, L), F32),
            pltpu.VMEM((2, 4, 2, 2, L, L), F32),
            dma((7,)), dma((7,)),
            dma((4,)), dma((4,)), dma((5,)), dma((5,)), dma, dma,
            dma((2,)), dma((2,)), dma((4, 2, NP)), dma((4, 2, NP)), dma((2, 2, NP)), dma((2, 2, NP)),
            dma((5, 2)), dma((5, 2)),
            dma((2, 8, 2, 2)), dma((2, 8, 2)), dma((2, 2, 2, 2, 2)),
            dma((2, 2, 2, 2, 2)), dma((2, 4, 2, 2)),
        ],
        compiler_params=pltpu.CompilerParams(
            collective_id=0, has_side_effects=True, vmem_limit_bytes=48 * 2**20
        ),
        cost_estimate=pl.CostEstimate(flops=2 * 17 * W * W * K * 3, bytes_accessed=2**20, transcendentals=W),
    )(dosage)


def solution(mesh):
    return jax.shard_map(
        body, mesh=mesh, in_specs=(P("samp", "var"),), out_specs=P("var", "samp"), check_vma=False
    )
```

```python
import jax
import jax.numpy as jnp
from jax import lax
from jax.experimental import pallas as pl
from jax.experimental.pallas import tpu as pltpu
from jax.sharding import PartitionSpec as P

MESH = pl.DeviceIdType.MESH
SAMPLES = 4096
VARIANTS = 8192
W = 256
K = 512
L = 128
NZ, NX = 8, 4
NP = 2
KP = K // NP
F32, BF16 = jnp.float32, jnp.bfloat16
STEPS = ((1, 0), (1, 1), (2, 0), (2, 1), (3, 0), (4, 0), (3, 1), (4, 1))
ORDER = (
    "H", "R0", "Y0", "M00", "O00", "F00", "Y1", "M01", "O01", "F01", "R1", "M10", "O10", "F10", "S00", "M11",
    "O11", "F11", "S01", "R2", "P0", "M20", "O20", "F20", "S10", "M21", "O21", "F21", "S11", "R3", "M30",
    "O30", "F30", "S20", "G00", "M31", "O31", "F31", "S21", "G01", "R4", "P1", "M40", "O40", "F40", "S30",
    "G10", "M41", "O41", "F41", "S31", "G11", "R5", "M50", "O50", "F50", "S40", "G20", "M51", "O51", "F51",
    "S41", "G21", "R6", "M60", "O60", "F60", "S50", "G30", "M61", "O61", "F61", "S51", "G31", "R7", "M70",
    "O70", "F70", "S60", "G40", "M71", "O71", "F71", "S61", "G41", "G50", "G51", "S70", "G60", "S71", "G61",
    "G70", "G71",
)


def split(a):
    hi = a.astype(BF16)
    return hi, (a - hi.astype(F32)).astype(BF16)


def kernel(
    x_ref, o_ref,
    stat_out, stat_in, stat, row_stat, cols, rows_in, relay, lhs, gram, part, half_in, full_in, y_in,
    stat_ss, stat_rs, zt_ss, zt_rs, st_ss, st_rs, rt_ss, rt_rs,
    row_ss, row_rs, z_ss, z_rs, far_ss, far_rs, sib_ss, sib_rs, x_ss, h_rs, f_rs, y_ss, y_rs,
):
    v, samp = lax.axis_index("var"), lax.axis_index("samp")
    z, yl, c = v // 4, (v // 2) % 2, v % 2
    yh, x = samp // 4, samp % 4

    def device(z=z, yl=yl, c=c, yh=yh, x=x):
        return (z * 4 + yl * 2 + c, yh * 4 + x)

    def remote(src, dst, ss, rs, to):
        return pltpu.make_async_remote_copy(
            src_ref=src, dst_ref=dst, send_sem=ss, recv_sem=rs, device_id=to, device_id_type=MESH
        )

    z_up, z_down = (z + 1) % NZ, (z + NZ - 1) % NZ
    x_right, x_left = (x + 1) % NX, (x + NX - 1) % NX
    sibling = device(c=1 - c)
    peers = [device(yh=(yh + k // 4) % 2, x=(x + k % 4) % NX) for k in range(1, 8)]
    others = [sibling, device(yl=1 - yl), device(yl=1 - yl, yh=1 - yh), device(z=z_up), device(z=z_down)]
    others += [device(z=(z + 2) % NZ), device(z=(z + 6) % NZ)]

    barrier = pltpu.get_barrier_semaphore()
    for to in peers + others:
        pl.semaphore_signal(barrier, inc=1, device_id=to, device_id_type=MESH)

    def raw(h, first=0, count=K):
        return cols.at[0, c, h, pl.ds(first, count)]

    def z_copy(dist, h, p):
        here = pl.ds(p * KP, KP)
        src = cols.at[dist, c, h, here] if dist else raw(h, p * KP, KP)
        return remote(
            src, cols.at[dist + 1, c, h, here], z_ss.at[dist, h, p], z_rs.at[dist, h, p], device(z=z_down)
        )

    def far_copy(hop, h, p):
        here = pl.ds(p * KP, KP)
        src = relay.at[h, here] if hop else raw(h, p * KP, KP)
        dst = cols.at[4, c, h, here] if hop else relay.at[h, here]
        return remote(src, dst, far_ss.at[hop, h, p], far_rs.at[hop, h, p], device(z=(z + 2) % NZ))

    def sib_copy(dist, h):
        there = cols.at[dist, c, h]
        return remote(there if dist else raw(h), there, sib_ss.at[dist, h], sib_rs.at[dist, h], sibling)

    def row_copy(h):
        return remote(raw(h), rows_in.at[h], row_ss.at[h], row_rs.at[h], device(yl=1 - yl))

    def z_stat(dist):
        return remote(
            stat.at[dist, c], stat.at[dist + 1, c], zt_ss.at[dist], zt_rs.at[dist], device(z=z_down)
        )

    def sib_stat(dist):
        return remote(stat.at[dist, c], stat.at[dist, c], st_ss.at[dist], st_rs.at[dist], sibling)

    row_stat_copy = remote(stat.at[0, c], row_stat, rt_ss, rt_rs, device(yl=1 - yl))

    def by_far(h, p):
        return h == 0 or p == 0

    dose = x_ref[...]
    for h in range(2):
        cols[0, c, h] = dose[:, h * L : (h + 1) * L]
    total = jnp.sum(dose, axis=0, keepdims=True)
    square = jnp.sum(dose * dose, axis=0, keepdims=True)
    line = lax.broadcasted_iota(jnp.int32, (8, W), 0)
    stat_out[...] = jnp.where(line == 0, total, jnp.where(line == 1, square, 0.0))
    stat_copies = [
        remote(stat_out, stat_in.at[k - 1], stat_ss.at[k - 1], stat_rs.at[k - 1], peers[k - 1])
        for k in range(1, 8)
    ]
    pl.semaphore_wait(barrier, len(peers) + len(others))
    for copy in stat_copies:
        copy.start()
    row_copy(0).start()
    for p in range(NP):
        z_copy(0, 0, p).start()
    for p in range(NP):
        far_copy(0, 0, p).start()
    for h in range(2):
        sib_copy(0, h).start()
    for copy in stat_copies:
        copy.wait_recv()
    sums = stat_out[...]
    for k in range(7):
        sums = sums + stat_in[k]
    mean = sums[0:1] / SAMPLES
    inv = lax.rsqrt(sums[1:2] / SAMPLES - mean * mean + 1e-06)
    stat[0, c] = jnp.where(line == 0, mean, inv)
    z_stat(0).start()
    row_stat_copy.start()
    sib_stat(0).start()
    row_copy(1).start()

    def put_rows(index, first, block):
        hi, lo = split(block)
        spot = (index, pl.ds(first, block.shape[0]))
        lhs[spot + (pl.ds(0, K),)] = hi
        lhs[spot + (pl.ds(K, K),)] = lo
        lhs[spot + (pl.ds(2 * K, K),)] = hi

    put_rows(yl, 0, ((dose - mean) * inv).T)

    def multiply(dist, h, p):
        right = []
        for c2 in range(2):
            of = stat[dist, c2, :, h * L : (h + 1) * L]
            right.append((cols[dist, c2, h] - of[0:1]) * of[1:2])
        hi, lo = split(jnp.concatenate(right, axis=1))
        right = jnp.concatenate([hi, hi, lo], axis=0)
        rows = pl.ds(p * L, L)
        for r in range(2):
            out = jnp.dot(lhs[r, rows], right, preferred_element_type=F32)
            gram[h, dist, r, 0, rows] = out[:, :L]
            gram[h, dist, r, 1, rows] = out[:, L:]

    row_id = lax.broadcasted_iota(jnp.int32, (L, L), 0)
    lane_id = lax.broadcasted_iota(jnp.int32, (L, L), 1)

    def tile(h, d, p):
        c2 = (c + d) % 2
        dist = (d - 2 * yl + c + 2) // 4
        r = (yl + 8 * 2 - (d - (c2 - c)) // 2) % 2
        return gram[h, dist, r, c2, pl.ds(p * L, L)]

    def build(h, s, p):
        above = lane_id + h * L > row_id + p * L
        part[h, s, p, 0] = jnp.where(above, tile(h, 2 * s, p), tile(h, 2 * s + 2, p))
        part[h, s, p, 1] = tile(h, 2 * s + 1, p)

    def role(s):
        return (s % 4 + NX - x) % NX

    def side(s):
        return (role(s) - 1) // 2

    def far_half(h, s, p, t):
        to = device(x=x_right if t == 0 else x_left)
        return remote(part.at[h, s, p, t], half_in.at[h, s, p], x_ss.at[h, s, p, t], h_rs.at[h, s, p], to)

    def near_copy(h, s, p, t):
        q = side(s)
        to = device(x=(x + 1 + 2 * q) % NX)
        return remote(
            part.at[h, s, p, t], full_in.at[h, s // 4, q, p, t], x_ss.at[h, s, p, t], f_rs.at[h, s // 4, q, p, t], to
        )

    def send_opposite(h, s, p):
        @pl.when(role(s) == 2)
        def _():
            build(h, s, p)
            far_half(h, s, p, 0).start()
            far_half(h, s, p, 1).start()

    def send_free(h, s, p):
        @pl.when(role(s) % 2 == 1)
        def _():
            build(h, s, p)
            near_copy(h, s, p, 1 - side(s)).start()

    def send_second(h, s, p):
        @pl.when(role(s) % 2 == 1)
        def _():
            t = side(s)
            far_half(h, s, p, 0).wait_recv()
            part[h, s, p, t] = part[h, s, p, t] + half_in[h, s, p]
            near_copy(h, s, p, t).start()

    def y_copy(h, s, yl2, p, t):
        me = 2 * yh + yl
        return remote(
            part.at[h, s, p, t], y_in.at[h, me, p, t], y_ss.at[h, s // 4, yl2, p, t], y_rs.at[h, me, p, t],
            device(yh=s // 4, yl=yl2),
        )

    def to_y(h, s, p, act):
        for yl2 in range(2):
            away = jnp.logical_or(s // 4 != yh, yl2 != yl)
            wanted = (yl + yl2 + s) % 2 == c

            @pl.when(away)
            def _():
                act(y_copy(h, s, yl2, p, 0))

            @pl.when(jnp.logical_and(away, wanted))
            def _():
                act(y_copy(h, s, yl2, p, 1))

    def collect(h, s, p):
        @pl.when(role(s) == 0)
        def _():
            build(h, s, p)
            for t in range(2):
                for q in range(2):
                    remote(
                        part.at[h, s, p, t], full_in.at[h, s // 4, q, p, t], x_ss.at[h, s, p, t],
                        f_rs.at[h, s // 4, q, p, t], device(x=x_right),
                    ).wait_recv()
                part[h, s, p, t] = part[h, s, p, t] + full_in[h, s // 4, 0, p, t] + full_in[h, s // 4, 1, p, t]
            to_y(h, s, p, lambda copy: copy.start())

            @pl.when(s // 4 == yh)
            def _():
                y_in[h, 2 * yh + yl, p] = part[h, s, p]

    def start_half():
        for p in range(NP):
            z_copy(0, 1, p).start()
            if by_far(1, p):
                far_copy(0, 1, p).start()

    def other_rows(p):
        if p == 0:
            row_stat_copy.wait_recv()
        row_copy(p).wait_recv()
        of = row_stat[:, p * L : (p + 1) * L]
        put_rows(1 - yl, p * L, ((rows_in[p] - of[0:1]) * of[1:2]).T)

    def receive(n):
        dist, h = STEPS[n]
        if h == 0:
            z_stat(dist - 1).wait_recv()
            if dist < 4:
                z_stat(dist).start()
            sib_stat(dist).start()
        for p in range(NP):
            if dist == 4 and by_far(h, p):
                far_copy(1, h, p).wait_recv()
            else:
                z_copy(dist - 1, h, p).wait_recv()
            if dist < 3 or (dist == 3 and not by_far(h, p)):
                z_copy(dist, h, p).start()
        sib_copy(dist, h).start()

    def pass_on(h):
        for p in range(NP):
            if by_far(h, p):
                far_copy(0, h, p).wait_recv()
                far_copy(1, h, p).start()

    def work(n, p):
        dist, h = STEPS[n]
        if p == 0:
            if dist == 1:
                if h == 0:
                    sib_stat(0).wait_recv()
                sib_copy(0, h).wait_recv()
            if h == 0:
                sib_stat(dist).wait_recv()
            sib_copy(dist, h).wait_recv()
        if dist == 1:
            multiply(0, h, p)
        multiply(dist, h, p)

    parts = dict(H=start_half, R=receive, P=pass_on, Y=other_rows, M=work)
    each = dict(O=send_opposite, F=send_free, S=send_second, G=collect)
    for event in ORDER:
        kind, digits = event[0], [int(digit) for digit in event[1:]]
        if kind in parts:
            parts[kind](*digits)
        else:
            dist, h = STEPS[digits[0]]
            for unit in (2 * dist - 2, 2 * dist - 1):
                each[kind](h, unit, digits[1])

    me = 2 * yh + yl
    first_yl = (yl + x) % 2
    mid_yl = (yl + x + c) % 2

    def landed(h, src, p, t):
        return remote(
            part.at[h, 0, p, t], y_in.at[h, src, p, t], y_ss.at[h, 0, 0, p, t], y_rs.at[h, src, p, t], sibling
        )

    row = lax.broadcasted_iota(jnp.int32, (L, 2 * W), 0)
    lane = lax.broadcasted_iota(jnp.int32, (L, 2 * W), 1)
    for p in range(2):
        pieces = [[None, None], [None, None]]
        for h in range(2):
            for src in range(4):
                @pl.when(me != src)
                def _():
                    landed(h, src, p, 0).wait_recv()

                    @pl.when((src % 2 + yl + x) % 2 == c)
                    def _():
                        landed(h, src, p, 1).wait_recv()

            upper = y_in[h, first_yl, p, 0] + y_in[h, 2 + first_yl, p, 0]
            lower = y_in[h, 1 - first_yl, p, 0] + y_in[h, 3 - first_yl, p, 0]
            pieces[0][h] = jnp.where(lane_id + h * L > row_id + p * L, upper, lower)
            pieces[1][h] = y_in[h, mid_yl, p, 1] + y_in[h, 2 + mid_yl, p, 1]
        band = jnp.concatenate(pieces[0] + pieces[1], axis=1) * (1.0 / 64.0)
        shift = row + (p * L + 1)
        for bit in range(9):
            moved = pltpu.roll(band, 2 * W - 2**bit, 1)
            band = jnp.where((shift & 2**bit) != 0, moved, band)
        reach = v * W + shift + samp * 2 * W + lane
        o_ref[p * L : (p + 1) * L] = jnp.where(reach < VARIANTS, band, 0.0)

    for copy in stat_copies:
        copy.wait_send()
    row_stat_copy.wait_send()
    for dist in range(5):
        if dist < 4:
            z_stat(dist).wait_send()
        sib_stat(dist).wait_send()
    for h in range(2):
        row_copy(h).wait_send()
        for p in range(NP):
            for dist in range(3):
                z_copy(dist, h, p).wait_send()
            if by_far(h, p):
                far_copy(0, h, p).wait_send()
                far_copy(1, h, p).wait_send()
            else:
                z_copy(3, h, p).wait_send()
        for dist in range(5):
            sib_copy(dist, h).wait_send()
        for s in range(8):
            @pl.when(role(s) != 0)
            def _():
                for p in range(2):
                    for t in range(2):
                        far_half(h, s, p, t).wait_send()

            @pl.when(role(s) == 0)
            def _():
                for p in range(2):
                    to_y(h, s, p, lambda copy: copy.wait_send())


def body(dosage):
    dma = pltpu.SemaphoreType.DMA
    return pl.pallas_call(
        kernel,
        out_shape=jax.ShapeDtypeStruct((W, 2 * W), F32),
        in_specs=[pl.BlockSpec(memory_space=pltpu.VMEM)],
        out_specs=pl.BlockSpec(memory_space=pltpu.VMEM),
        scratch_shapes=[
            pltpu.VMEM((8, W), F32),
            pltpu.VMEM((7, 8, W), F32),
            pltpu.VMEM((5, 2, 8, W), F32),
            pltpu.VMEM((8, W), F32),
            pltpu.VMEM((5, 2, 2, K, L), F32),
            pltpu.VMEM((2, K, L), F32),
            pltpu.VMEM((2, K, L), F32),
            pltpu.VMEM((2, W, 3 * K), BF16),
            pltpu.VMEM((2, 5, 2, 2, W, L), F32),
            pltpu.VMEM((2, 8, 2, 2, L, L), F32),
            pltpu.VMEM((2, 8, 2, L, L), F32),
            pltpu.VMEM((2, 2, 2, 2, 2, L, L), F32),
            pltpu.VMEM((2, 4, 2, 2, L, L), F32),
            dma((7,)), dma((7,)),
            dma((4,)), dma((4,)), dma((5,)), dma((5,)), dma, dma,
            dma((2,)), dma((2,)), dma((4, 2, NP)), dma((4, 2, NP)), dma((2, 2, NP)), dma((2, 2, NP)),
            dma((5, 2)), dma((5, 2)),
            dma((2, 8, 2, 2)), dma((2, 8, 2)), dma((2, 2, 2, 2, 2)),
            dma((2, 2, 2, 2, 2)), dma((2, 4, 2, 2)),
        ],
        compiler_params=pltpu.CompilerParams(
            collective_id=0, has_side_effects=True, vmem_limit_bytes=48 * 2**20
        ),
        cost_estimate=pl.CostEstimate(flops=2 * 17 * W * W * K * 3, bytes_accessed=2**20, transcendentals=W),
    )(dosage)


def solution(mesh):
    return jax.shard_map(
        body, mesh=mesh, in_specs=(P("samp", "var"),), out_specs=P("var", "samp"), check_vma=False
    )
```

```python
import jax
import jax.numpy as jnp
from jax import lax
from jax.experimental import pallas as pl
from jax.experimental.pallas import tpu as pltpu
from jax.sharding import PartitionSpec as P

MESH = pl.DeviceIdType.MESH
SAMPLES = 4096
VARIANTS = 8192
W = 256
K = 512
L = 128
NZ, NX = 8, 4
NP = 2
KP = K // NP
F32, BF16 = jnp.float32, jnp.bfloat16
STEPS = ((1, 0), (1, 1), (2, 0), (2, 1), (3, 0), (4, 0), (3, 1), (4, 1))
ORDER = (
    "H", "R0", "Y0", "M00", "O00", "F00", "Y1", "M01", "O01", "F01", "R1", "M10", "O10", "F10", "S00", "M11",
    "O11", "F11", "S01", "R2", "P0", "M20", "O20", "F20", "S10", "M21", "O21", "F21", "S11", "R3", "M30",
    "O30", "F30", "S20", "G00", "M31", "O31", "F31", "S21", "G01", "R4", "P1", "M40", "O40", "F40", "S30",
    "G10", "M41", "O41", "F41", "S31", "G11", "R5", "M50", "O50", "F50", "S40", "G20", "M51", "O51", "F51",
    "S41", "G21", "R6", "M60", "O60", "F60", "S50", "G30", "M61", "O61", "F61", "S51", "G31", "R7", "M70",
    "O70", "F70", "S60", "G40", "M71", "O71", "F71", "S61", "G41", "G50", "G51", "S70", "G60", "S71", "G61",
    "G70", "G71",
)


def split(a):
    hi = a.astype(BF16)
    return hi, (a - hi.astype(F32)).astype(BF16)


def kernel(
    x_ref, o_ref,
    stat_out, stat_in, stat, row_stat, cols, rows_in, relay, lhs, gram, part, half_in, full_in, y_in,
    stat_ss, stat_rs, zt_ss, zt_rs, st_ss, st_rs, rt_ss, rt_rs,
    row_ss, row_rs, z_ss, z_rs, far_ss, far_rs, sib_ss, sib_rs, x_ss, h_rs, f_rs, y_ss, y_rs,
):
    v, samp = lax.axis_index("var"), lax.axis_index("samp")
    z, yl, c = v // 4, (v // 2) % 2, v % 2
    yh, x = samp // 4, samp % 4

    def device(z=z, yl=yl, c=c, yh=yh, x=x):
        return (z * 4 + yl * 2 + c, yh * 4 + x)

    def remote(src, dst, ss, rs, to):
        return pltpu.make_async_remote_copy(
            src_ref=src, dst_ref=dst, send_sem=ss, recv_sem=rs, device_id=to, device_id_type=MESH
        )

    z_up, z_down = (z + 1) % NZ, (z + NZ - 1) % NZ
    x_right, x_left = (x + 1) % NX, (x + NX - 1) % NX
    sibling = device(c=1 - c)
    peers = [device(yh=(yh + k // 4) % 2, x=(x + k % 4) % NX) for k in range(1, 8)]
    others = [sibling, device(yl=1 - yl), device(yl=1 - yl, yh=1 - yh), device(z=z_up), device(z=z_down)]
    others += [device(z=(z + 2) % NZ), device(z=(z + 6) % NZ)]

    barrier = pltpu.get_barrier_semaphore()
    for to in peers + others:
        pl.semaphore_signal(barrier, inc=1, device_id=to, device_id_type=MESH)

    def raw(h, first=0, count=K):
        return cols.at[0, c, h, pl.ds(first, count)]

    def z_copy(dist, h, p):
        here = pl.ds(p * KP, KP)
        src = cols.at[dist, c, h, here] if dist else raw(h, p * KP, KP)
        return remote(
            src, cols.at[dist + 1, c, h, here], z_ss.at[dist, h, p], z_rs.at[dist, h, p], device(z=z_down)
        )

    def far_copy(hop, h, p):
        here = pl.ds(p * KP, KP)
        src = relay.at[h, here] if hop else raw(h, p * KP, KP)
        dst = cols.at[4, c, h, here] if hop else relay.at[h, here]
        return remote(src, dst, far_ss.at[hop, h, p], far_rs.at[hop, h, p], device(z=(z + 2) % NZ))

    def sib_copy(dist, h):
        there = cols.at[dist, c, h]
        return remote(there if dist else raw(h), there, sib_ss.at[dist, h], sib_rs.at[dist, h], sibling)

    def row_copy(h):
        return remote(raw(h), rows_in.at[h], row_ss.at[h], row_rs.at[h], device(yl=1 - yl))

    def z_stat(dist):
        return remote(
            stat.at[dist, c], stat.at[dist + 1, c], zt_ss.at[dist], zt_rs.at[dist], device(z=z_down)
        )

    def sib_stat(dist):
        return remote(stat.at[dist, c], stat.at[dist, c], st_ss.at[dist], st_rs.at[dist], sibling)

    row_stat_copy = remote(stat.at[0, c], row_stat, rt_ss, rt_rs, device(yl=1 - yl))

    def by_far(h, p):
        return h == 0 or p == 0

    dose = x_ref[...]
    for h in range(2):
        cols[0, c, h] = dose[:, h * L : (h + 1) * L]
    total = jnp.sum(dose, axis=0, keepdims=True)
    square = jnp.sum(dose * dose, axis=0, keepdims=True)
    line = lax.broadcasted_iota(jnp.int32, (8, W), 0)
    stat_out[...] = jnp.where(line == 0, total, jnp.where(line == 1, square, 0.0))
    stat_copies = [
        remote(stat_out, stat_in.at[k - 1], stat_ss.at[k - 1], stat_rs.at[k - 1], peers[k - 1])
        for k in range(1, 8)
    ]
    pl.semaphore_wait(barrier, len(peers) + len(others))
    for copy in stat_copies:
        copy.start()
    row_copy(0).start()
    for p in range(NP):
        z_copy(0, 0, p).start()
    for p in range(NP):
        far_copy(0, 0, p).start()
    for h in range(2):
        sib_copy(0, h).start()
    for copy in stat_copies:
        copy.wait_recv()
    sums = stat_out[...]
    for k in range(7):
        sums = sums + stat_in[k]
    mean = sums[0:1] / SAMPLES
    inv = lax.rsqrt(sums[1:2] / SAMPLES - mean * mean + 1e-06)
    stat[0, c] = jnp.where(line == 0, mean, inv)
    z_stat(0).start()
    row_stat_copy.start()
    sib_stat(0).start()
    row_copy(1).start()

    def put_rows(index, first, block):
        hi, lo = split(block)
        spot = (index, pl.ds(first, block.shape[0]))
        lhs[spot + (pl.ds(0, K),)] = hi
        lhs[spot + (pl.ds(K, K),)] = lo
        lhs[spot + (pl.ds(2 * K, K),)] = hi

    put_rows(yl, 0, ((dose - mean) * inv).T)

    def multiply(dist, h, p):
        right = []
        for c2 in range(2):
            of = stat[dist, c2, :, h * L : (h + 1) * L]
            right.append((cols[dist, c2, h] - of[0:1]) * of[1:2])
        hi, lo = split(jnp.concatenate(right, axis=1))
        right = jnp.concatenate([hi, hi, lo], axis=0)
        rows = pl.ds(p * L, L)
        for r in range(2):
            out = jnp.dot(lhs[r, rows], right, preferred_element_type=F32)
            gram[h, dist, r, 0, rows] = out[:, :L]
            gram[h, dist, r, 1, rows] = out[:, L:]

    row_id = lax.broadcasted_iota(jnp.int32, (L, L), 0)
    lane_id = lax.broadcasted_iota(jnp.int32, (L, L), 1)

    def tile(h, d, p):
        c2 = (c + d) % 2
        dist = (d - 2 * yl + c + 2) // 4
        r = (yl + 8 * 2 - (d - (c2 - c)) // 2) % 2
        return gram[h, dist, r, c2, pl.ds(p * L, L)]

    def build(h, s, p):
        above = lane_id + h * L > row_id + p * L
        part[h, s, p, 0] = jnp.where(above, tile(h, 2 * s, p), tile(h, 2 * s + 2, p))
        part[h, s, p, 1] = tile(h, 2 * s + 1, p)

    def role(s):
        return (s % 4 + NX - x) % NX

    def side(s):
        return (role(s) - 1) // 2

    def far_half(h, s, p, t):
        to = device(x=x_right if t == 0 else x_left)
        return remote(part.at[h, s, p, t], half_in.at[h, s, p], x_ss.at[h, s, p, t], h_rs.at[h, s, p], to)

    def near_copy(h, s, p, t):
        q = side(s)
        to = device(x=(x + 1 + 2 * q) % NX)
        return remote(
            part.at[h, s, p, t], full_in.at[h, s // 4, q, p, t], x_ss.at[h, s, p, t], f_rs.at[h, s // 4, q, p, t], to
        )

    def send_opposite(h, s, p):
        @pl.when(role(s) == 2)
        def _():
            build(h, s, p)
            far_half(h, s, p, 0).start()
            far_half(h, s, p, 1).start()

    def send_free(h, s, p):
        @pl.when(role(s) % 2 == 1)
        def _():
            build(h, s, p)
            near_copy(h, s, p, 1 - side(s)).start()

    def send_second(h, s, p):
        @pl.when(role(s) % 2 == 1)
        def _():
            t = side(s)
            far_half(h, s, p, 0).wait_recv()
            part[h, s, p, t] = part[h, s, p, t] + half_in[h, s, p]
            near_copy(h, s, p, t).start()

    def y_copy(h, s, yl2, p, t):
        me = 2 * yh + yl
        return remote(
            part.at[h, s, p, t], y_in.at[h, me, p, t], y_ss.at[h, s // 4, yl2, p, t], y_rs.at[h, me, p, t],
            device(yh=s // 4, yl=yl2),
        )

    def to_y(h, s, p, act, only=None):
        for yl2 in range(2):
            away = jnp.logical_or(s // 4 != yh, yl2 != yl)
            wanted = (yl + yl2 + s) % 2 == c

            if only != 1:
                @pl.when(away)
                def _():
                    act(y_copy(h, s, yl2, p, 0))

            if only != 0:
                @pl.when(jnp.logical_and(away, wanted))
                def _():
                    act(y_copy(h, s, yl2, p, 1))

    def collect(h, s, p):
        @pl.when(role(s) == 0)
        def _():
            build(h, s, p)
            for t in range(2):
                for q in range(2):
                    remote(
                        part.at[h, s, p, t], full_in.at[h, s // 4, q, p, t], x_ss.at[h, s, p, t],
                        f_rs.at[h, s // 4, q, p, t], device(x=x_right),
                    ).wait_recv()
                part[h, s, p, t] = part[h, s, p, t] + full_in[h, s // 4, 0, p, t] + full_in[h, s // 4, 1, p, t]
                to_y(h, s, p, lambda copy: copy.start(), t)

            @pl.when(s // 4 == yh)
            def _():
                y_in[h, 2 * yh + yl, p] = part[h, s, p]

    def start_half():
        for p in range(NP):
            z_copy(0, 1, p).start()
            if by_far(1, p):
                far_copy(0, 1, p).start()

    def other_rows(p):
        if p == 0:
            row_stat_copy.wait_recv()
        row_copy(p).wait_recv()
        of = row_stat[:, p * L : (p + 1) * L]
        put_rows(1 - yl, p * L, ((rows_in[p] - of[0:1]) * of[1:2]).T)

    def receive(n):
        dist, h = STEPS[n]
        if h == 0:
            z_stat(dist - 1).wait_recv()
            if dist < 4:
                z_stat(dist).start()
            sib_stat(dist).start()
        for p in range(NP):
            if dist == 4 and by_far(h, p):
                far_copy(1, h, p).wait_recv()
            else:
                z_copy(dist - 1, h, p).wait_recv()
            if dist < 3 or (dist == 3 and not by_far(h, p)):
                z_copy(dist, h, p).start()
        sib_copy(dist, h).start()

    def pass_on(h):
        for p in range(NP):
            if by_far(h, p):
                far_copy(0, h, p).wait_recv()
                far_copy(1, h, p).start()

    def work(n, p):
        dist, h = STEPS[n]
        if p == 0:
            if dist == 1:
                if h == 0:
                    sib_stat(0).wait_recv()
                sib_copy(0, h).wait_recv()
            if h == 0:
                sib_stat(dist).wait_recv()
            sib_copy(dist, h).wait_recv()
        if dist == 1:
            multiply(0, h, p)
        multiply(dist, h, p)

    parts = dict(H=start_half, R=receive, P=pass_on, Y=other_rows, M=work)
    each = dict(O=send_opposite, F=send_free, S=send_second, G=collect)
    for event in ORDER:
        kind, digits = event[0], [int(digit) for digit in event[1:]]
        if kind in parts:
            parts[kind](*digits)
        else:
            dist, h = STEPS[digits[0]]
            for unit in (2 * dist - 2, 2 * dist - 1):
                each[kind](h, unit, digits[1])

    me = 2 * yh + yl
    first_yl = (yl + x) % 2
    mid_yl = (yl + x + c) % 2

    def landed(h, src, p, t):
        return remote(
            part.at[h, 0, p, t], y_in.at[h, src, p, t], y_ss.at[h, 0, 0, p, t], y_rs.at[h, src, p, t], sibling
        )

    row = lax.broadcasted_iota(jnp.int32, (L, 2 * W), 0)
    lane = lax.broadcasted_iota(jnp.int32, (L, 2 * W), 1)
    for p in range(2):
        pieces = [[None, None], [None, None]]
        for h in range(2):
            for src in range(4):
                @pl.when(me != src)
                def _():
                    landed(h, src, p, 0).wait_recv()

                    @pl.when((src % 2 + yl + x) % 2 == c)
                    def _():
                        landed(h, src, p, 1).wait_recv()

            upper = y_in[h, first_yl, p, 0] + y_in[h, 2 + first_yl, p, 0]
            lower = y_in[h, 1 - first_yl, p, 0] + y_in[h, 3 - first_yl, p, 0]
            pieces[0][h] = jnp.where(lane_id + h * L > row_id + p * L, upper, lower)
            pieces[1][h] = y_in[h, mid_yl, p, 1] + y_in[h, 2 + mid_yl, p, 1]
        band = jnp.concatenate(pieces[0] + pieces[1], axis=1) * (1.0 / 64.0)
        shift = row + (p * L + 1)
        for bit in range(9):
            moved = pltpu.roll(band, 2 * W - 2**bit, 1)
            band = jnp.where((shift & 2**bit) != 0, moved, band)
        reach = v * W + shift + samp * 2 * W + lane
        o_ref[p * L : (p + 1) * L] = jnp.where(reach < VARIANTS, band, 0.0)

    for copy in stat_copies:
        copy.wait_send()
    row_stat_copy.wait_send()
    for dist in range(5):
        if dist < 4:
            z_stat(dist).wait_send()
        sib_stat(dist).wait_send()
    for h in range(2):
        row_copy(h).wait_send()
        for p in range(NP):
            for dist in range(3):
                z_copy(dist, h, p).wait_send()
            if by_far(h, p):
                far_copy(0, h, p).wait_send()
                far_copy(1, h, p).wait_send()
            else:
                z_copy(3, h, p).wait_send()
        for dist in range(5):
            sib_copy(dist, h).wait_send()
        for s in range(8):
            @pl.when(role(s) != 0)
            def _():
                for p in range(2):
                    for t in range(2):
                        far_half(h, s, p, t).wait_send()

            @pl.when(role(s) == 0)
            def _():
                for p in range(2):
                    to_y(h, s, p, lambda copy: copy.wait_send())


def body(dosage):
    dma = pltpu.SemaphoreType.DMA
    return pl.pallas_call(
        kernel,
        out_shape=jax.ShapeDtypeStruct((W, 2 * W), F32),
        in_specs=[pl.BlockSpec(memory_space=pltpu.VMEM)],
        out_specs=pl.BlockSpec(memory_space=pltpu.VMEM),
        scratch_shapes=[
            pltpu.VMEM((8, W), F32),
            pltpu.VMEM((7, 8, W), F32),
            pltpu.VMEM((5, 2, 8, W), F32),
            pltpu.VMEM((8, W), F32),
            pltpu.VMEM((5, 2, 2, K, L), F32),
            pltpu.VMEM((2, K, L), F32),
            pltpu.VMEM((2, K, L), F32),
            pltpu.VMEM((2, W, 3 * K), BF16),
            pltpu.VMEM((2, 5, 2, 2, W, L), F32),
            pltpu.VMEM((2, 8, 2, 2, L, L), F32),
            pltpu.VMEM((2, 8, 2, L, L), F32),
            pltpu.VMEM((2, 2, 2, 2, 2, L, L), F32),
            pltpu.VMEM((2, 4, 2, 2, L, L), F32),
            dma((7,)), dma((7,)),
            dma((4,)), dma((4,)), dma((5,)), dma((5,)), dma, dma,
            dma((2,)), dma((2,)), dma((4, 2, NP)), dma((4, 2, NP)), dma((2, 2, NP)), dma((2, 2, NP)),
            dma((5, 2)), dma((5, 2)),
            dma((2, 8, 2, 2)), dma((2, 8, 2)), dma((2, 2, 2, 2, 2)),
            dma((2, 2, 2, 2, 2)), dma((2, 4, 2, 2)),
        ],
        compiler_params=pltpu.CompilerParams(
            collective_id=0, has_side_effects=True, vmem_limit_bytes=48 * 2**20
        ),
        cost_estimate=pl.CostEstimate(flops=2 * 17 * W * W * K * 3, bytes_accessed=2**20, transcendentals=W),
    )(dosage)


def solution(mesh):
    return jax.shard_map(
        body, mesh=mesh, in_specs=(P("samp", "var"),), out_specs=P("var", "samp"), check_vma=False
    )
```
